128 devices in a mesh: dp: 16 (over x, y), tensor: 8 (over z, core).
Axes of the slice: x: 4, y: 4, z: 4, core: 2. Of those that a mesh axis runs over, the one named last changes fastest.
Arguments:
- teacher_hidden: bfloat16 [2048, 4096], P('dp'), may hold values from -70 to 70
- student_hidden: bfloat16 [2048, 4096], P('dp'), may hold values from -70 to 70
- teacher_head: bfloat16 [4096, 76288], P(None, ('dp', 'tensor')), may hold values from -0.25 to 0.25
- student_head: bfloat16 [4096, 76288], P(None, ('dp', 'tensor')), may hold values from -0.25 to 0.25
- sampled_ids: int32 [2048], replicated, may hold values from 0 to 76287
- valid_mask: int32 [2048], replicated, may hold values 0 or 1
Outputs:
- head_grad: bfloat16 [4096, 76288], P(None, ('dp', 'tensor'))
- reverse_kl: float32 [], replicated
The draws below stay inside these ranges and needn't reach their ends.
All inputs are finite; a program needn't handle non-finite values.
Results may differ from the reference program's by a relative error of at most 0.0075.
Values may be sent and summed in bfloat16 or wider, within the bound.
No kernel may reach another device: no remote copies, remote signals or barrier semaphores. Data moves between devices by JAX's collectives and lax.ppermute only.
A program may use at most 192 MiB of HBM per device.

```python
import jax
import jax.numpy as jnp
from jax import lax

D = 4096
TOKENS = 2048
VOCAB = 76288


def draw_teacher_hidden(key, part):
    key = jax.random.fold_in(key, 11)
    value_key = jax.random.fold_in(key, 0)
    values = jnp.clip(jax.random.normal(value_key, (TOKENS, D), jnp.float32), -6.0, 6.0)
    return values.astype(jnp.bfloat16)


def draw_student_hidden(key, part):
    key = jax.random.fold_in(key, 12)
    value_key = jax.random.fold_in(key, 0)
    values = jnp.clip(jax.random.normal(value_key, (TOKENS, D), jnp.float32), -6.0, 6.0)
    return values.astype(jnp.bfloat16)


def plant(array, key, least, largest):
    index_at = [jax.random.randint(jax.random.fold_in(key, axis), (), 0, length) for axis, length in enumerate(array.shape)]
    longest = array.shape.index(max(array.shape))
    next_to = index_at[:longest] + [(index_at[longest] + 1) % array.shape[longest]] + index_at[longest + 1:]
    return array.at[tuple(index_at)].set(least).at[tuple(next_to)].set(largest)


def level_of(stream_key, dims, cuts, smallest, top_value):
    factor_of, own = 1.0, jax.random.fold_in(stream_key, 6)
    for dim, blocks in cuts:
        heights = jnp.exp(jax.random.uniform(jax.random.fold_in(own, dim), (blocks,), jnp.float32, smallest / len(cuts), top_value / len(cuts)))
        factor_of = factor_of * jnp.repeat(heights, dims[dim] // blocks).reshape([-1 if axis == dim else 1 for axis in range(len(dims))])
    return factor_of


def gaussian(rng, dims, spread, most, shards=(), kind=jnp.bfloat16):
    entries = jax.random.normal(rng, dims, jnp.float32) * spread
    if len(shards) > 0:
        entries = level_of(rng, dims, shards, -0.22, 0.18) * entries
    return jnp.clip(entries, min=-most, max=most).astype(kind)


def setup_inputs(seed: int = 0) -> dict:
    seeds = jax.random.split(jax.random.key(seed), 7)
    return {
        "teacher_hidden": draw_teacher_hidden(jax.random.fold_in(seeds[6], 71), 0),
        "student_hidden": draw_student_hidden(jax.random.fold_in(seeds[6], 71), 0),
        "teacher_head": gaussian(seeds[2], (D, VOCAB), (D / 9) ** -0.5, 0.25, ((1, 128),)),
        "student_head": gaussian(seeds[3], (D, VOCAB), (D / 9) ** -0.5, 0.25, ((1, 128),)),
        "sampled_ids": plant(jax.random.randint(seeds[4], (TOKENS,), 0, VOCAB), jax.random.fold_in(seeds[4], 1), 0, VOCAB - 1).astype(jnp.int32),
        "valid_mask": plant((jax.random.randint(seeds[5], (TOKENS,), 0, 4) < 3).astype(jnp.int32), jax.random.fold_in(seeds[5], 1), 0, 1),
    }


loss_scale = 64.0
sampled_weight = 0.0625

def logit_gradient(factor, student_prob, difference, divergence, advantage, chosen):
    onehot = chosen.astype(jnp.float32)
    inner = student_prob * (difference - divergence[:, None])
    inner = inner - sampled_weight * advantage[:, None] * (onehot - student_prob)
    return (factor[:, None] * inner).astype(jnp.bfloat16)

def reference(teacher_hidden, student_hidden, teacher_head, student_head, sampled_ids, valid_mask):
    teacher_logits = jnp.dot(teacher_hidden, teacher_head, preferred_element_type=jnp.float32)
    student_logits = jnp.dot(student_hidden, student_head, preferred_element_type=jnp.float32)
    teacher_norm = jax.nn.logsumexp(teacher_logits, axis=1)
    student_norm = jax.nn.logsumexp(student_logits, axis=1)
    student_logp = student_logits - student_norm[:, None]
    difference = student_logp - (teacher_logits - teacher_norm[:, None])
    student_prob = jnp.exp(student_logp)
    divergence = lax.optimization_barrier(jnp.sum(student_prob * difference, axis=1))
    vocab_index = jnp.arange(teacher_logits.shape[1], dtype=jnp.int32)
    chosen = sampled_ids[:, None] == vocab_index[None, :]
    advantage = lax.optimization_barrier(jnp.sum(jnp.where(chosen, -difference, jnp.float32(0.0)), axis=1))
    weights = valid_mask.astype(jnp.float32)
    token_count = jnp.sum(weights)
    factor = loss_scale * weights / jnp.sqrt(token_count)
    logit_grad = logit_gradient(factor, student_prob, difference, divergence, advantage, chosen)
    head_grad = lax.dot_general(student_hidden, logit_grad, (((0,), (0,)), ((), ())), preferred_element_type=jnp.float32).astype(jnp.bfloat16)
    reverse_kl = jnp.sum(weights * divergence) / token_count
    return (head_grad, reverse_kl)
```

```python
import functools

import jax
import jax.numpy as jnp
from jax import lax
from jax.experimental import pallas as pl
from jax.experimental.pallas import tpu as pltpu
from jax.sharding import PartitionSpec as P

LOSS_SCALE = 64.0
SAMPLED_WEIGHT = 0.0625
SIDE = 4
AXES = ("dp", "tensor")
OFFSETS = (0, -1, 1, 2)
F32 = jnp.float32
MIB = 1 << 20


def flat(x, y, z, c):
    return (((x % SIDE) * SIDE + y % SIDE) * SIDE + z % SIDE) * 2 + c


def pairs(step):
    return [
        (flat(x, y, z, c), flat(*step(x, y, z, c)))
        for x in range(SIDE) for y in range(SIDE) for z in range(SIDE) for c in range(2)
    ]


def first(d):
    return pairs(lambda x, y, z, c: (x + d * (1 - c), y + d * c, z, c))


def second(d):
    return pairs(lambda x, y, z, c: (x + d * c, y + d * (1 - c), z, c))


def along(axis, d):
    return pairs(lambda x, y, z, c: (x + d * (axis == 0), y + d * (axis == 1), z + d * (axis == 2), c))


SIBLING = pairs(lambda x, y, z, c: (x, y, z, 1 - c))


def send(array, perm):
    return lax.ppermute(array, AXES, perm)


def nt(a, b):
    return lax.dot_general(a, b, (((1,), (1,)), ((), ())), preferred_element_type=F32)


def stats_of(s, t, chosen):
    u = s - t
    ms = jnp.max(s, axis=0, keepdims=True)
    mt = jnp.max(t, axis=0, keepdims=True)
    es = jnp.exp(s - ms)
    zs = jnp.sum(es, axis=0, keepdims=True)
    zt = jnp.sum(jnp.exp(t - mt), axis=0, keepdims=True)
    mean = jnp.sum(es * u, axis=0, keepdims=True) / zs
    picked = jnp.sum(jnp.where(chosen, u, 0.0), axis=0, keepdims=True)
    return u, (mt + jnp.log(zt), ms + jnp.log(zs), mean, picked)


def add_all(values):
    if len(values) == 4:
        return (values[0] + values[3]) + (values[1] + values[2])
    return sum(values[1:], values[0])


def join(parts):
    def lse(values):
        top = functools.reduce(jnp.maximum, values)
        return top + jnp.log(add_all([jnp.exp(v - top) for v in values]))
    nt_all = lse([p[0] for p in parts])
    ns_all = lse([p[1] for p in parts])
    mean = add_all([jnp.exp(p[1] - ns_all) * p[2] for p in parts])
    return nt_all, ns_all, mean, add_all([p[3] for p in parts])


def logits_kernel(steps, first_ref, ids_ref, t_ref, s_ref, ta_ref, sa_ref, tb_ref, sb_ref,
                  oas_ref, oau_ref, obs_ref, obu_ref, st_ref):
    k = pl.program_id(0)
    t_hid = t_ref[0] if len(t_ref.shape) == 3 else t_ref[...]
    s_hid = s_ref[0] if len(s_ref.shape) == 3 else s_ref[...]
    for head, hid, out in ((sa_ref, s_hid, oas_ref), (ta_ref, t_hid, oau_ref),
                           (sb_ref, s_hid, obs_ref), (tb_ref, t_hid, obu_ref)):
        part = nt(head[...], hid)

        @pl.when(k == 0)
        def _():
            out[...] = part

        @pl.when(k > 0)
        def _():
            out[...] += part

    @pl.when(k == steps - 1)
    def _():
        parts = []
        for i, (so, uo) in enumerate(((oas_ref, oau_ref), (obs_ref, obu_ref))):
            s, t = so[...], uo[...]
            rows = lax.broadcasted_iota(jnp.int32, s.shape, 0) + first_ref[i]
            u, part = stats_of(s, t, rows == ids_ref[...])
            uo[...] = u
            parts.append(part)
        total = join(parts)
        tokens = total[0].shape[1] // SIDE
        for q in range(4):
            for b in range(SIDE):
                st_ref[b, q:q + 1, :] = total[q][:, b * tokens:(b + 1) * tokens]


def logits_call(firsts, ids, stack, heads, t_alone=None, s_alone=None):
    ta, sa, tb, sb = heads
    vocab, depth = ta.shape
    tile = 1024
    steps = depth // tile
    if t_alone is None:
        tokens = stack.shape[1]
        hids = [stack, stack]
        hid_specs = [pl.BlockSpec((1, tokens, tile), lambda k, j=j: (j, 0, k)) for j in range(2)]
    else:
        tokens = t_alone.shape[0]
        hids = [t_alone, s_alone]
        hid_specs = [pl.BlockSpec((tokens, tile), lambda k: (0, k))] * 2
    head_spec = pl.BlockSpec((vocab, tile), lambda k: (0, k))
    out = jax.ShapeDtypeStruct((vocab, tokens), F32)
    whole = pl.BlockSpec((vocab, tokens), lambda k: (0, 0))
    return pl.pallas_call(
        functools.partial(logits_kernel, steps),
        grid=(steps,),
        in_specs=[pl.BlockSpec(memory_space=pltpu.SMEM), pl.BlockSpec((1, tokens), lambda k: (0, 0))]
        + hid_specs + [head_spec] * 4,
        out_specs=[whole] * 4 + [pl.BlockSpec((SIDE, 4, tokens // SIDE), lambda k: (0, 0, 0))],
        out_shape=[out] * 4 + [jax.ShapeDtypeStruct((SIDE, 4, tokens // SIDE), F32)],
        compiler_params=pltpu.CompilerParams(vmem_limit_bytes=32 * MIB),
        cost_estimate=pl.CostEstimate(flops=8 * vocab * tokens * depth, bytes_accessed=8 * vocab * depth, transcendentals=0),
    )(firsts, ids, *hids, ta, sa, tb, sb)


def order_kernel(place_ref, *refs):
    *groups, out_ref = refs
    for j, group in enumerate(groups):
        for i in range(SIDE):
            b = place_ref[j * SIDE + i]
            for q in range(4):
                out_ref[q, pl.ds(b, 1), :] = group[i, q:q + 1, :]


def order_call(place, groups):
    tokens = groups[0].shape[-1]
    return pl.pallas_call(
        order_kernel,
        in_specs=[pl.BlockSpec(memory_space=pltpu.SMEM)] + [pl.BlockSpec(memory_space=pltpu.VMEM)] * len(groups),
        out_specs=pl.BlockSpec(memory_space=pltpu.VMEM),
        out_shape=jax.ShapeDtypeStruct((4, SIDE * SIDE, tokens), F32),
    )(place, *groups)


def join_kernel(*refs):
    *ins, out_ref = refs
    total = join([[r[q] for q in range(4)] for r in ins])
    for q in range(4):
        out_ref[q] = total[q]


def join_call(parts):
    vmem = pl.BlockSpec(memory_space=pltpu.VMEM)
    return pl.pallas_call(
        join_kernel,
        in_specs=[vmem] * len(parts),
        out_specs=vmem,
        out_shape=jax.ShapeDtypeStruct(parts[0].shape, F32),
    )(*parts)


def finish_kernel(place_ref, factor_ref, weight_ref, *refs):
    *ins, coef_ref, kl_ref, rows_ref = refs
    n_t, n_s, mean, picked = join([[r[q] for q in range(4)] for r in ins])
    kl_ref[...] = jnp.sum(weight_ref[...] * (mean + n_t - n_s), keepdims=True)
    pull = SAMPLED_WEIGHT * -(picked + n_t - n_s)
    for q, value in enumerate((n_s, factor_ref[...], pull - mean, pull)):
        rows_ref[q] = value
    tokens = n_s.shape[1]
    for j in range(SIDE):
        for q in range(4):
            for i in range(SIDE):
                coef_ref[j, q:q + 1, i * tokens:(i + 1) * tokens] = rows_ref[q, pl.ds(place_ref[j * SIDE + i], 1), :]


def finish_call(place, factor, weight, parts):
    vmem = pl.BlockSpec(memory_space=pltpu.VMEM)
    tokens = factor.shape[1]
    return pl.pallas_call(
        finish_kernel,
        in_specs=[pl.BlockSpec(memory_space=pltpu.SMEM)] + [vmem] * (2 + len(parts)),
        out_specs=[vmem, vmem],
        out_shape=[jax.ShapeDtypeStruct((SIDE, 4, SIDE * tokens), F32), jax.ShapeDtypeStruct((1, 1), F32)],
        scratch_shapes=[pltpu.VMEM((4, SIDE * SIDE, tokens), F32)],
    )(place, factor, weight, *parts)


def grad_kernel(first_ref, ids_ref, coef_ref, *refs):
    *ins, out_ref = refs
    for j in range(SIDE):
        s, u = ins[2 * j][...], ins[2 * j + 1][...]
        n_s, factor, shift, pull = (coef_ref[j, q:q + 1, :] for q in range(4))
        rows = lax.broadcasted_iota(jnp.int32, s.shape, 0) + first_ref[0]
        inner = jnp.exp(s - n_s) * (u + shift)
        inner = inner - jnp.where(rows == ids_ref[j:j + 1, :], pull, 0.0)
        tokens = s.shape[1]
        out_ref[:, j * tokens:(j + 1) * tokens] = (factor * inner).astype(jnp.bfloat16)


def grad_call(first_row, ids, coef, logits):
    vocab, tokens = logits[0].shape
    vmem = pl.BlockSpec(memory_space=pltpu.VMEM)
    return pl.pallas_call(
        grad_kernel,
        in_specs=[pl.BlockSpec(memory_space=pltpu.SMEM)] + [vmem] * (2 + len(logits)),
        out_specs=vmem,
        out_shape=jax.ShapeDtypeStruct((vocab, SIDE * tokens), jnp.bfloat16),
        compiler_params=pltpu.CompilerParams(vmem_limit_bytes=32 * MIB),
        cost_estimate=pl.CostEstimate(flops=10 * vocab * tokens * SIDE, bytes_accessed=10 * vocab * tokens * SIDE, transcendentals=0),
    )(first_row, ids, coef, *logits)


def head_kernel(ga_ref, gb_ref, *refs):
    *hids, out_ref = refs
    half = len(hids) // 2
    total = None
    for g, group in ((ga_ref, hids[:half]), (gb_ref, hids[half:])):
        rows = jnp.concatenate([r[0] if len(r.shape) == 3 else r[...] for r in group], axis=0)
        part = jnp.dot(g[...], rows, preferred_element_type=F32)
        total = part if total is None else total + part
    out_ref[...] = total.astype(jnp.bfloat16)


def head_call(ga, gb, hids):
    vocab, tokens = ga.shape
    depth = hids[0].shape[-1]
    tile = 512
    specs = []
    for h in hids:
        if h.ndim == 3:
            specs.append(pl.BlockSpec((1, h.shape[1], tile), lambda i: (1, 0, i)))
        else:
            specs.append(pl.BlockSpec((h.shape[0], tile), lambda i: (0, i)))
    whole = pl.BlockSpec((vocab, tokens), lambda i: (0, 0))
    return pl.pallas_call(
        head_kernel,
        grid=(depth // tile,),
        in_specs=[whole, whole] + specs,
        out_specs=pl.BlockSpec((vocab, tile), lambda i: (0, i)),
        out_shape=jax.ShapeDtypeStruct((vocab, depth), jnp.bfloat16),
        compiler_params=pltpu.CompilerParams(vmem_limit_bytes=32 * MIB),
        cost_estimate=pl.CostEstimate(flops=4 * vocab * tokens * depth, bytes_accessed=4 * tokens * depth, transcendentals=0),
    )(ga, gb, *hids)


def local(teacher_hidden, student_hidden, teacher_head, student_head, sampled_ids, valid_mask):
    dp, tensor = lax.axis_index("dp"), lax.axis_index("tensor")
    x, y, core = dp // SIDE, dp % SIDE, tensor % 2
    half = teacher_hidden.shape[0] // 2
    vocab = teacher_head.shape[1]

    ta, sa = teacher_head.T, student_head.T
    tb, sb = send(ta, SIBLING), send(sa, SIBLING)
    heads = (ta, sa, tb, sb)

    shift = jnp.array([o % SIDE for o in OFFSETS], jnp.int32)
    one = (jnp.where(core == 0, x, y) + shift) % SIDE
    two = (jnp.where(core == 0, y, x) + shift) % SIDE
    place = jnp.where(core == 0, one[None, :] * SIDE + two[:, None], two[:, None] * SIDE + one[None, :]).reshape(-1)

    def mine(a):
        return lax.dynamic_index_in_dim(a.reshape(SIDE * SIDE, 2, half), core, 1, keepdims=False)

    ids = jnp.take(mine(sampled_ids), place, axis=0).reshape(SIDE, SIDE * half)
    all_weights = valid_mask.astype(F32)
    token_count = jnp.sum(all_weights)
    weights = mine(all_weights)
    factor = LOSS_SCALE * weights / jnp.sqrt(token_count)
    row_of = flat(x, y, tensor // 2, core) * vocab
    other_of = flat(x, y, tensor // 2, 1 - core) * vocab
    firsts = jnp.stack([row_of, other_of])

    own = lax.dynamic_slice_in_dim(jnp.stack([teacher_hidden, student_hidden]), core * half, half, 1)
    low, high = send(own, first(1)), send(own, first(-1))
    far_t, far_s = send(low[0], first(1)), send(high[1], first(-1))
    far = jnp.stack([far_t, far_s])
    row = jnp.concatenate([own, low, high, far], axis=1)
    row_low, row_high = send(row, second(1)), send(row, second(-1))
    far_t, far_s = send(row_low[0], second(1)), send(row_high[1], second(-1))

    groups = [
        logits_call(firsts, ids[0:1], row, heads),
        logits_call(firsts, ids[1:2], row_low, heads),
        logits_call(firsts, ids[2:3], row_high, heads),
        logits_call(firsts, ids[3:4], None, heads, far_t, far_s),
    ]
    students = [row, row_low, row_high, far_s]
    others = [send(h, SIBLING) for h in students]

    total = order_call(place, [g[4] for g in groups])
    for axis in range(3):
        parts = [total, send(total, along(axis, 1)), send(total, along(axis, -1)), send(total, along(axis, 2))]
        if axis < 2:
            total = join_call(parts)
    coef, kl = finish_call(place, factor, weights, parts)

    away = grad_call(firsts[1:], ids, coef, [a for g in groups for a in g[2:4]])
    arrived = send(away, SIBLING)
    kl = kl + send(kl, SIBLING)
    kept = grad_call(firsts[:1], ids, coef, [a for g in groups for a in g[0:2]])
    head_grad = head_call(kept, arrived, students + others).T
    return head_grad, kl[0, 0] / token_count


def solution(mesh):
    placed = (
        P("dp", None),
        P("dp", None),
        P(None, AXES),
        P(None, AXES),
        P(),
        P(),
    )
    return jax.shard_map(
        local,
        mesh=mesh,
        in_specs=placed,
        out_specs=(P(None, AXES), P()),
        check_vma=False,
    )
```

```python
import functools

import jax
import jax.numpy as jnp
from jax import lax
from jax.experimental import pallas as pl
from jax.experimental.pallas import tpu as pltpu
from jax.sharding import PartitionSpec as P

LOSS_SCALE = 64.0
SAMPLED_WEIGHT = 0.0625
SIDE = 4
AXES = ("dp", "tensor")
OFFSETS = (0, -1, 1, 2)
F32 = jnp.float32
MIB = 1 << 20


def flat(x, y, z, c):
    return (((x % SIDE) * SIDE + y % SIDE) * SIDE + z % SIDE) * 2 + c


def pairs(step):
    return [
        (flat(x, y, z, c), flat(*step(x, y, z, c)))
        for x in range(SIDE) for y in range(SIDE) for z in range(SIDE) for c in range(2)
    ]


def first(d):
    return pairs(lambda x, y, z, c: (x + d * (1 - c), y + d * c, z, c))


def second(d):
    return pairs(lambda x, y, z, c: (x + d * c, y + d * (1 - c), z, c))


def along(axis, d):
    return pairs(lambda x, y, z, c: (x + d * (axis == 0), y + d * (axis == 1), z + d * (axis == 2), c))


SIBLING = pairs(lambda x, y, z, c: (x, y, z, 1 - c))


def send(array, perm):
    return lax.ppermute(array, AXES, perm)


def nt(a, b):
    return lax.dot_general(a, b, (((1,), (1,)), ((), ())), preferred_element_type=F32)


def stats_of(s, t, chosen):
    u = s - t
    ms = jnp.max(s, axis=0, keepdims=True)
    mt = jnp.max(t, axis=0, keepdims=True)
    es = jnp.exp(s - ms)
    zs = jnp.sum(es, axis=0, keepdims=True)
    zt = jnp.sum(jnp.exp(t - mt), axis=0, keepdims=True)
    mean = jnp.sum(es * u, axis=0, keepdims=True) / zs
    picked = jnp.sum(jnp.where(chosen, u, 0.0), axis=0, keepdims=True)
    return u, (mt + jnp.log(zt), ms + jnp.log(zs), mean, picked)


def add_all(values):
    if len(values) == 4:
        return (values[0] + values[3]) + (values[1] + values[2])
    return sum(values[1:], values[0])


def join(parts):
    def lse(values):
        top = functools.reduce(jnp.maximum, values)
        return top + jnp.log(add_all([jnp.exp(v - top) for v in values]))
    nt_all = lse([p[0] for p in parts])
    ns_all = lse([p[1] for p in parts])
    mean = add_all([jnp.exp(p[1] - ns_all) * p[2] for p in parts])
    return nt_all, ns_all, mean, add_all([p[3] for p in parts])


def logits_kernel(first_ref, ids_ref, t_ref, s_ref, ta_ref, sa_ref, tb_ref, sb_ref, *refs):
    *_, out_ref, st_ref, held, sems = refs
    parts, copies = [], []
    for i, (sh, th) in enumerate(((sa_ref, ta_ref), (sb_ref, tb_ref))):
        held[2 * i] = nt(sh[...], s_ref[...])
        held[2 * i + 1] = nt(th[...], t_ref[...])
        s, t = held[2 * i], held[2 * i + 1]
        rows = lax.broadcasted_iota(jnp.int32, s.shape, 0) + first_ref[i]
        u, part = stats_of(s, t, rows == ids_ref[...])
        held[2 * i + 1] = u
        parts.append(part)
        copies.append(pltpu.make_async_copy(held.at[pl.ds(2 * i, 2)], out_ref.at[pl.ds(2 * i, 2)], sems.at[i]))
        copies[-1].start()
    total = join(parts)
    tokens = total[0].shape[1] // SIDE
    for q in range(4):
        for b in range(SIDE):
            st_ref[b, q:q + 1, :] = total[q][:, b * tokens:(b + 1) * tokens]
    for copy in copies:
        copy.wait()


def logits_call(firsts, ids, t_hid, s_hid, heads, after=()):
    vocab, depth = heads[0].shape
    tokens = t_hid.shape[0]
    vmem = pl.BlockSpec(memory_space=pltpu.VMEM)
    return pl.pallas_call(
        logits_kernel,
        in_specs=[pl.BlockSpec(memory_space=pltpu.SMEM)] + [vmem] * 7 + [pl.BlockSpec(memory_space=pl.ANY)] * len(after),
        out_specs=[pl.BlockSpec(memory_space=pltpu.HBM), vmem],
        out_shape=[
            pltpu.HBM((4, vocab, tokens), F32),
            jax.ShapeDtypeStruct((SIDE, 4, tokens // SIDE), F32),
        ],
        scratch_shapes=[pltpu.VMEM((4, vocab, tokens), F32), pltpu.SemaphoreType.DMA((2,))],
        compiler_params=pltpu.CompilerParams(vmem_limit_bytes=20 * MIB),
        cost_estimate=pl.CostEstimate(flops=8 * vocab * tokens * depth, bytes_accessed=8 * vocab * depth, transcendentals=0),
    )(firsts, ids, t_hid, s_hid, *heads, *after)


def order_kernel(place_ref, *refs):
    *groups, out_ref = refs
    for j, group in enumerate(groups):
        for i in range(SIDE):
            b = place_ref[j * SIDE + i]
            for q in range(4):
                out_ref[q, pl.ds(b, 1), :] = group[i, q:q + 1, :]


SMALL = pltpu.CompilerParams(vmem_limit_bytes=4 * MIB)


def order_call(place, groups):
    tokens = groups[0].shape[-1]
    return pl.pallas_call(
        order_kernel,
        in_specs=[pl.BlockSpec(memory_space=pltpu.SMEM)] + [pl.BlockSpec(memory_space=pltpu.VMEM)] * len(groups),
        out_specs=pl.BlockSpec(memory_space=pltpu.VMEM),
        out_shape=jax.ShapeDtypeStruct((4, SIDE * SIDE, tokens), F32),
        compiler_params=SMALL,
    )(place, *groups)


def join_kernel(*refs):
    *ins, out_ref = refs
    total = join([[r[q] for q in range(4)] for r in ins])
    for q in range(4):
        out_ref[q] = total[q]


def join_call(parts):
    vmem = pl.BlockSpec(memory_space=pltpu.VMEM)
    return pl.pallas_call(
        join_kernel,
        in_specs=[vmem] * len(parts),
        out_specs=vmem,
        out_shape=jax.ShapeDtypeStruct(parts[0].shape, F32),
        compiler_params=SMALL,
    )(*parts)


def finish_kernel(place_ref, factor_ref, weight_ref, *refs):
    *ins, coef_ref, kl_ref, rows_ref = refs
    n_t, n_s, mean, picked = join([[r[q] for q in range(4)] for r in ins])
    kl_ref[...] = jnp.sum(weight_ref[...] * (mean + n_t - n_s), keepdims=True)
    pull = SAMPLED_WEIGHT * -(picked + n_t - n_s)
    for q, value in enumerate((n_s, factor_ref[...], pull - mean, pull)):
        rows_ref[q] = value
    tokens = n_s.shape[1]
    for j in range(SIDE):
        for q in range(4):
            for i in range(SIDE):
                coef_ref[j, q:q + 1, i * tokens:(i + 1) * tokens] = rows_ref[q, pl.ds(place_ref[j * SIDE + i], 1), :]


def finish_call(place, factor, weight, parts):
    vmem = pl.BlockSpec(memory_space=pltpu.VMEM)
    tokens = factor.shape[1]
    return pl.pallas_call(
        finish_kernel,
        in_specs=[pl.BlockSpec(memory_space=pltpu.SMEM)] + [vmem] * (2 + len(parts)),
        out_specs=[vmem, vmem],
        out_shape=[jax.ShapeDtypeStruct((SIDE, 4, SIDE * tokens), F32), jax.ShapeDtypeStruct((1, 1), F32)],
        scratch_shapes=[pltpu.VMEM((4, SIDE * SIDE, tokens), F32)],
        compiler_params=SMALL,
    )(place, factor, weight, *parts)


def grad_kernel(part, first_ref, ids_ref, coef_ref, *refs):
    *ins, out_ref, held, sems = refs
    copies = [pltpu.make_async_copy(ref.at[pl.ds(2 * part, 2)], held.at[j], sems.at[j]) for j, ref in enumerate(ins)]
    for copy in copies:
        copy.start()
    tokens = held.shape[3]
    for j in range(SIDE):
        copies[j].wait()
        s, u = held[j, 0], held[j, 1]
        n_s, factor, shift, pull = (coef_ref[j, q:q + 1, :] for q in range(4))
        rows = lax.broadcasted_iota(jnp.int32, s.shape, 0) + first_ref[part]
        inner = jnp.exp(s - n_s) * (u + shift)
        inner = inner - jnp.where(rows == ids_ref[j:j + 1, :], pull, 0.0)
        out_ref[:, j * tokens:(j + 1) * tokens] = (factor * inner).astype(jnp.bfloat16)


def grad_call(part, firsts, ids, coef, logits):
    _, vocab, tokens = logits[0].shape
    vmem = pl.BlockSpec(memory_space=pltpu.VMEM)
    return pl.pallas_call(
        functools.partial(grad_kernel, part),
        in_specs=[pl.BlockSpec(memory_space=pltpu.SMEM), vmem, vmem] + [pl.BlockSpec(memory_space=pltpu.HBM)] * SIDE,
        out_specs=vmem,
        out_shape=jax.ShapeDtypeStruct((vocab, SIDE * tokens), jnp.bfloat16),
        scratch_shapes=[pltpu.VMEM((SIDE, 2, vocab, tokens), F32), pltpu.SemaphoreType.DMA((SIDE,))],
        compiler_params=pltpu.CompilerParams(vmem_limit_bytes=16 * MIB),
        cost_estimate=pl.CostEstimate(flops=10 * vocab * tokens * SIDE, bytes_accessed=10 * vocab * tokens * SIDE, transcendentals=0),
    )(firsts, ids, coef, *[pltpu.with_memory_space_constraint(a, pltpu.HBM) for a in logits])


def head_kernel(ga_ref, gb_ref, *refs):
    *hids, out_ref = refs
    half = len(hids) // 2
    total = None
    for g, group in ((ga_ref, hids[:half]), (gb_ref, hids[half:])):
        rows = jnp.concatenate([r[0] if len(r.shape) == 3 else r[...] for r in group], axis=0)
        part = jnp.dot(g[...], rows, preferred_element_type=F32)
        total = part if total is None else total + part
    out_ref[...] = total.astype(jnp.bfloat16)


def head_call(ga, gb, hids):
    vocab, tokens = ga.shape
    depth = hids[0].shape[-1]
    tile = 512
    specs = []
    for h in hids:
        if h.ndim == 3:
            specs.append(pl.BlockSpec((1, h.shape[1], tile), lambda i: (1, 0, i)))
        else:
            specs.append(pl.BlockSpec((h.shape[0], tile), lambda i: (0, i)))
    whole = pl.BlockSpec((vocab, tokens), lambda i: (0, 0))
    return pl.pallas_call(
        head_kernel,
        grid=(depth // tile,),
        in_specs=[whole, whole] + specs,
        out_specs=pl.BlockSpec((vocab, tile), lambda i: (0, i)),
        out_shape=jax.ShapeDtypeStruct((vocab, depth), jnp.bfloat16),
        compiler_params=pltpu.CompilerParams(vmem_limit_bytes=16 * MIB),
        cost_estimate=pl.CostEstimate(flops=4 * vocab * tokens * depth, bytes_accessed=4 * tokens * depth, transcendentals=0),
    )(ga, gb, *[pltpu.with_memory_space_constraint(a, pltpu.HBM) for a in hids])


def local(teacher_hidden, student_hidden, teacher_head, student_head, sampled_ids, valid_mask):
    dp, tensor = lax.axis_index("dp"), lax.axis_index("tensor")
    x, y, core = dp // SIDE, dp % SIDE, tensor % 2
    half = teacher_hidden.shape[0] // 2
    vocab = teacher_head.shape[1]

    ta, sa = teacher_head.T, student_head.T
    tb, sb = send(ta, SIBLING), send(sa, SIBLING)

    shift = jnp.array([o % SIDE for o in OFFSETS], jnp.int32)
    one = (jnp.where(core == 0, x, y) + shift) % SIDE
    two = (jnp.where(core == 0, y, x) + shift) % SIDE
    place = jnp.where(core == 0, one[None, :] * SIDE + two[:, None], two[:, None] * SIDE + one[None, :]).reshape(-1)

    def mine(a):
        return lax.dynamic_index_in_dim(a.reshape(SIDE * SIDE, 2, half), core, 1, keepdims=False)

    ids = jnp.take(mine(sampled_ids), place, axis=0).reshape(SIDE, SIDE * half)
    all_weights = valid_mask.astype(F32)
    token_count = jnp.sum(all_weights)
    weights = mine(all_weights)
    factor = LOSS_SCALE * weights / jnp.sqrt(token_count)
    row_of = flat(x, y, tensor // 2, core) * vocab
    other_of = flat(x, y, tensor // 2, 1 - core) * vocab
    firsts = jnp.stack([row_of, other_of])

    own = lax.dynamic_slice_in_dim(jnp.stack([teacher_hidden, student_hidden]), core * half, half, 1)
    low, high = send(own, first(1)), send(own, first(-1))
    far_t, far_s = send(low[0], first(1)), send(high[1], first(-1))
    far_t, far_s, tb, sb = lax.optimization_barrier((far_t, far_s, tb, sb))
    heads = (ta, sa, tb, sb)
    row_t = jnp.concatenate([own[0], low[0], high[0], far_t], axis=0)
    row_s = jnp.concatenate([own[1], low[1], high[1], far_s], axis=0)
    low_t, high_s = send(row_t, second(1)), send(row_s, second(-1))
    high_t, low_s = send(row_t, second(-1)), send(row_s, second(1))
    group0 = logits_call(firsts, ids[0:1], row_t, row_s, heads)
    other0 = send(row_s, SIBLING)
    low_t, high_s, other0, *group0 = lax.optimization_barrier((low_t, high_s, other0, *group0))
    far_t, far_s = send(low_t, second(1)), send(high_s, second(-1))
    other1, other2 = send(low_s, SIBLING), send(high_s, SIBLING)
    group1 = logits_call(firsts, ids[1:2], low_t, low_s, heads)
    group2 = logits_call(firsts, ids[2:3], high_t, high_s, heads)
    group3 = logits_call(firsts, ids[3:4], far_t, far_s, heads, (group1[1], group2[1], other1, other2))
    other3 = send(far_s, SIBLING)
    groups = [group0, group1, group2, group3]
    students = [row_s, low_s, high_s, far_s]
    others = [other0, other1, other2, other3]

    total = order_call(place, [g[1] for g in groups])
    for axis in range(3):
        parts = [total, send(total, along(axis, 1)), send(total, along(axis, -1)), send(total, along(axis, 2))]
        if axis < 2:
            total = join_call(parts)
    coef, kl = finish_call(place, factor, weights, parts)

    logits = [g[0] for g in groups]
    away = grad_call(1, firsts, ids, coef, logits)
    arrived = send(away, SIBLING)
    kept = grad_call(0, firsts, ids, coef, logits)
    kl = kl + send(kl, SIBLING)
    head_grad = head_call(kept, arrived, students + others).T
    return head_grad, kl[0, 0] / token_count


def solution(mesh):
    placed = (
        P("dp", None),
        P("dp", None),
        P(None, AXES),
        P(None, AXES),
        P(),
        P(),
    )
    return jax.shard_map(
        local,
        mesh=mesh,
        in_specs=placed,
        out_specs=(P(None, AXES), P()),
        check_vma=False,
    )
```

```python
import functools

import jax
import jax.numpy as jnp
from jax import lax
from jax.experimental import pallas as pl
from jax.experimental.pallas import tpu as pltpu
from jax.sharding import PartitionSpec as P

LOSS_SCALE = 64.0
SAMPLED_WEIGHT = 0.0625
SIDE = 4
AXES = ("dp", "tensor")
OFFSETS = (0, -1, 1, 2)
F32 = jnp.float32
MIB = 1 << 20


def flat(x, y, z, c):
    return (((x % SIDE) * SIDE + y % SIDE) * SIDE + z % SIDE) * 2 + c


def pairs(step):
    return [
        (flat(x, y, z, c), flat(*step(x, y, z, c)))
        for x in range(SIDE) for y in range(SIDE) for z in range(SIDE) for c in range(2)
    ]


def first(d):
    return pairs(lambda x, y, z, c: (x + d * (1 - c), y + d * c, z, c))


def second(d):
    return pairs(lambda x, y, z, c: (x + d * c, y + d * (1 - c), z, c))


def along(axis, d):
    return pairs(lambda x, y, z, c: (x + d * (axis == 0), y + d * (axis == 1), z + d * (axis == 2), c))


def z_pair():
    return pairs(lambda x, y, z, c: (x, y, z + 1 - 2 * c, c))


SIBLING = pairs(lambda x, y, z, c: (x, y, z, 1 - c))


def send(array, perm):
    return lax.ppermute(array, AXES, perm)


def nt(a, b):
    return lax.dot_general(a, b, (((1,), (1,)), ((), ())), preferred_element_type=F32)


PAD = -1e30


def stats_of(held, i, first, ids):
    rows, tokens = held.shape[1:]
    step = 40

    def chunk(j, r):
        return held[j, pl.ds(pl.multiple_of(r * step, 8), step), :].reshape(step // 8, 8, tokens)

    def tops(r, carry):
        ms, mt = carry
        return jnp.maximum(ms, jnp.max(chunk(2 * i, r), axis=0)), jnp.maximum(mt, jnp.max(chunk(2 * i + 1, r), axis=0))

    low = jnp.full((8, tokens), PAD, F32)
    ms, mt = lax.fori_loop(0, rows // step, tops, (low, low))
    ms, mt = jnp.max(ms, axis=0, keepdims=True), jnp.max(mt, axis=0, keepdims=True)
    at = lax.broadcasted_iota(jnp.int32, (step, tokens), 0).reshape(step // 8, 8, tokens)
    wanted = ids - first

    def sums(r, carry):
        s, t = chunk(2 * i, r), chunk(2 * i + 1, r)
        u = s - t
        es = jnp.exp(s - ms)
        et = jnp.exp(t - mt)
        picked = jnp.where(at == wanted - r * step, u, 0.0)
        return tuple(c + jnp.sum(v, axis=0) for c, v in zip(carry, (es, et, es * u, picked)))

    nil = jnp.zeros((8, tokens), F32)
    zs, zt, mean, picked = (
        jnp.sum(v, axis=0, keepdims=True) for v in lax.fori_loop(0, rows // step, sums, (nil,) * 4))
    return mt + jnp.log(zt), ms + jnp.log(zs), mean / zs, picked


def add_all(values):
    if len(values) == 4:
        return (values[0] + values[3]) + (values[1] + values[2])
    return sum(values[1:], values[0])


def join(parts):
    def lse(values):
        top = functools.reduce(jnp.maximum, values)
        return top + jnp.log(add_all([jnp.exp(v - top) for v in values]))
    nt_all = lse([p[0] for p in parts])
    ns_all = lse([p[1] for p in parts])
    mean = add_all([jnp.exp(p[1] - ns_all) * p[2] for p in parts])
    return nt_all, ns_all, mean, add_all([p[3] for p in parts])


def logits_kernel(shape, scalar_ref, ids_ref, *refs):
    n = len(shape)
    count = sum(len(kind) for group in shape for kind in group)
    pieces, heads, refs = list(refs[:count]), refs[count:count + 4], refs[count + 4:]
    hidden = [[[pieces.pop(0) for _ in kind] for kind in group] for group in shape]
    *outs, student_ref = refs[-7 - 2 * n:-6]
    hid, head, held, in_sems, head_sems, out_sems = refs[-6:]
    vocab, rows = head.shape[1], held.shape[2]
    common, width = hidden[0][0][0].shape[-1], hidden[0][1][0].shape[-1]
    at = (0, pl.multiple_of(common + scalar_ref[2] * width, width), pl.multiple_of(common + (1 - scalar_ref[2]) * width, width))

    def fetch(g, kind, j):
        found = hidden[g][kind]
        source = found[j] if len(found) == 2 else found[0].at[(j,) if len(found[0].shape) == 3 else (g, j)]
        return pltpu.make_async_copy(source, hid.at[g, j, :, pl.ds(at[kind], source.shape[-1])], in_sems.at[g, kind, j])

    def fetch_head(h, lo, hi, sem):
        return pltpu.make_async_copy(heads[h].at[:, lo:hi], head.at[h, :, lo:hi], head_sems.at[sem])

    depth = hid.shape[3]
    early = [fetch_head(0, 0, common, 4)] + [fetch(g, 0, 1) for g in range(n)]
    late = [fetch_head(0, common, depth, 0)] + [fetch(g, kind, 1) for g in range(n) for kind in (1, 2)]
    teacher = [fetch_head(1, 0, depth, 1)] + [fetch(g, kind, 0) for g in range(n) for kind in (0, 1, 2)]
    sibling = [[fetch_head(2, 0, depth, 2)], [fetch_head(3, 0, depth, 3)]]

    def start(copies):
        for copy in copies:
            copy.start()

    def wait(copies):
        for copy in copies:
            copy.wait()

    start(early)
    start(late)
    wait(early)
    start(teacher)
    for g in range(n):
        held[g, 0, :vocab, :] = nt(head[0, :, :common], hid[g, 1, :, :common])
    wait(late)
    start(sibling[0])
    for g in range(n):
        held[g, 0, :vocab, :] += nt(head[0, :, common:], hid[g, 1, :, common:])
    wait(teacher)
    start(sibling[1])
    kept = [
        pltpu.make_async_copy(hid.at[g, 1], student_ref.at[pl.ds(g * hid.shape[2], hid.shape[2])], out_sems.at[g, 2])
        for g in range(n)
    ]
    start(kept)
    for g in range(n):
        held[g, 1, :vocab, :] = nt(head[1], hid[g, 0])
    parts, stored = [[] for _ in range(n)], []

    def finish(i):
        for g in range(n):
            held[g, 2 * i:2 * i + 2, vocab:, :] = jnp.full((2, rows - vocab, held.shape[3]), PAD, F32)
            stored.append(pltpu.make_async_copy(
                held.at[g, pl.ds(2 * i, 2)], outs[2 * g].at[pl.ds(2 * i, 2)], out_sems.at[g, i]))
            stored[-1].start()
            parts[g].append(stats_of(held.at[g], i, scalar_ref[i], ids_ref[g:g + 1, :]))

    finish(0)
    for i in range(2):
        wait(sibling[i])
        for g in range(n):
            held[g, 2 + i, :vocab, :] = nt(head[2 + i], hid[g, 1 - i])
    finish(1)
    for g in range(n):
        total = join(parts[g])
        tokens = total[0].shape[1] // SIDE
        for q in range(4):
            for b in range(SIDE):
                outs[2 * g + 1][b, q:q + 1, :] = total[q][:, b * tokens:(b + 1) * tokens]
    wait(kept)
    wait(stored)


def logits_call(scalars, ids, groups, heads, after=()):
    vocab, depth = heads[0].shape
    n, tokens = ids.shape
    rows = -(-vocab // 40) * 40
    vmem, hbm = pl.BlockSpec(memory_space=pltpu.VMEM), pl.BlockSpec(memory_space=pl.ANY)
    pieces = [a for group in groups for kind in group for a in kind]
    shape = [[[None] * len(kind) for kind in group] for group in groups]
    out = pl.pallas_call(
        functools.partial(logits_kernel, shape),
        in_specs=[pl.BlockSpec(memory_space=pltpu.SMEM), vmem] + [hbm] * (len(pieces) + 4 + len(after)),
        out_specs=[pl.BlockSpec(memory_space=pltpu.HBM), vmem] * n + [pl.BlockSpec(memory_space=pltpu.HBM)],
        out_shape=[
            pltpu.HBM((4, rows, tokens), F32),
            jax.ShapeDtypeStruct((SIDE, 4, tokens // SIDE), F32),
        ] * n + [pltpu.HBM((n * tokens, depth), jnp.bfloat16)],
        scratch_shapes=[
            pltpu.VMEM((n, 2, tokens, depth), jnp.bfloat16),
            pltpu.VMEM((4, vocab, depth), jnp.bfloat16),
            pltpu.VMEM((n, 4, rows, tokens), F32),
            pltpu.SemaphoreType.DMA((n, 3, 2)),
            pltpu.SemaphoreType.DMA((5,)),
            pltpu.SemaphoreType.DMA((n, 3)),
        ],
        compiler_params=pltpu.CompilerParams(vmem_limit_bytes=(26 + 9 * n) * MIB),
        cost_estimate=pl.CostEstimate(flops=8 * n * vocab * tokens * depth, bytes_accessed=8 * vocab * depth, transcendentals=0),
    )(scalars, ids, *pieces, *in_hbm(heads), *after)
    return *[out[2 * g:2 * g + 2] for g in range(n)], out[-1]


def order_kernel(place_ref, *refs):
    *groups, out_ref = refs
    for j, group in enumerate(groups):
        for i in range(SIDE):
            b = place_ref[j * SIDE + i]
            for q in range(4):
                out_ref[q, pl.ds(b, 1), :] = group[i, q:q + 1, :]


SMALL = pltpu.CompilerParams(vmem_limit_bytes=4 * MIB)


def order_call(place, groups):
    tokens = groups[0].shape[-1]
    return pl.pallas_call(
        order_kernel,
        in_specs=[pl.BlockSpec(memory_space=pltpu.SMEM)] + [pl.BlockSpec(memory_space=pltpu.VMEM)] * len(groups),
        out_specs=pl.BlockSpec(memory_space=pltpu.VMEM),
        out_shape=jax.ShapeDtypeStruct((4, SIDE * SIDE, tokens), F32),
        compiler_params=SMALL,
    )(place, *groups)


def join_kernel(*refs):
    *ins, out_ref = refs
    total = join([[r[q] for q in range(4)] for r in ins])
    for q in range(4):
        out_ref[q] = total[q]


def join_call(parts):
    vmem = pl.BlockSpec(memory_space=pltpu.VMEM)
    return pl.pallas_call(
        join_kernel,
        in_specs=[vmem] * len(parts),
        out_specs=vmem,
        out_shape=jax.ShapeDtypeStruct(parts[0].shape, F32),
        compiler_params=SMALL,
    )(*parts)


def finish_kernel(place_ref, factor_ref, weight_ref, *refs):
    *ins, coef_ref, kl_ref, rows_ref = refs
    n_t, n_s, mean, picked = join([[r[q] for q in range(4)] for r in ins])
    kl_ref[...] = jnp.sum(weight_ref[...] * (mean + n_t - n_s), keepdims=True)
    pull = SAMPLED_WEIGHT * -(picked + n_t - n_s)
    for q, value in enumerate((n_s, factor_ref[...], pull - mean, pull)):
        rows_ref[q] = value
    tokens = n_s.shape[1]
    for j in range(SIDE):
        for q in range(4):
            for i in range(SIDE):
                coef_ref[j, q:q + 1, i * tokens:(i + 1) * tokens] = rows_ref[q, pl.ds(place_ref[j * SIDE + i], 1), :]


def finish_call(place, factor, weight, parts):
    vmem = pl.BlockSpec(memory_space=pltpu.VMEM)
    tokens = factor.shape[1]
    return pl.pallas_call(
        finish_kernel,
        in_specs=[pl.BlockSpec(memory_space=pltpu.SMEM)] + [vmem] * (2 + len(parts)),
        out_specs=[vmem, vmem],
        out_shape=[jax.ShapeDtypeStruct((SIDE, 4, SIDE * tokens), F32), jax.ShapeDtypeStruct((1, 1), F32)],
        scratch_shapes=[pltpu.VMEM((4, SIDE * SIDE, tokens), F32)],
        compiler_params=SMALL,
    )(place, factor, weight, *parts)


def grad_kernel(part, scalar_ref, ids_ref, coef_ref, *refs):
    *ins, out_ref, held, sems = refs
    vocab = out_ref.shape[0]
    copies = [pltpu.make_async_copy(ref.at[pl.ds(2 * part, 2)], held.at[j], sems.at[j]) for j, ref in enumerate(ins)]
    for copy in copies:
        copy.start()
    tokens = held.shape[3]
    for j in range(SIDE):
        copies[j].wait()
        s, t = held[j, 0], held[j, 1]
        n_s, factor, shift, pull = (coef_ref[j, q:q + 1, :] for q in range(4))
        rows = lax.broadcasted_iota(jnp.int32, s.shape, 0)
        inner = jnp.exp(s - n_s) * (s - t + shift)
        inner = inner - jnp.where(rows == ids_ref[j:j + 1, :] - scalar_ref[part], pull, 0.0)
        out_ref[:, j * tokens:(j + 1) * tokens] = (factor * inner).astype(jnp.bfloat16)[:vocab]


def in_hbm(arrays):
    return [pltpu.with_memory_space_constraint(a, pltpu.HBM) for a in arrays]


def grad_call(part, scalars, ids, coef, logits, vocab):
    _, rows, tokens = logits[0].shape
    vmem, hbm = pl.BlockSpec(memory_space=pltpu.VMEM), pl.BlockSpec(memory_space=pltpu.HBM)
    return pl.pallas_call(
        functools.partial(grad_kernel, part),
        in_specs=[pl.BlockSpec(memory_space=pltpu.SMEM), vmem, vmem] + [hbm] * SIDE,
        out_specs=vmem,
        out_shape=jax.ShapeDtypeStruct((vocab, SIDE * tokens), jnp.bfloat16),
        scratch_shapes=[pltpu.VMEM((SIDE, 2, rows, tokens), F32), pltpu.SemaphoreType.DMA((SIDE,))],
        compiler_params=pltpu.CompilerParams(vmem_limit_bytes=16 * MIB),
        cost_estimate=pl.CostEstimate(flops=10 * vocab * tokens * SIDE, bytes_accessed=10 * vocab * tokens * SIDE, transcendentals=0),
    )(scalars, ids, coef, *in_hbm(logits))


def head_kernel(ga_ref, gb_ref, *refs):
    *hids, out_ref = refs
    half = len(hids) // 2
    total = None
    for g, group in ((ga_ref, hids[:half]), (gb_ref, hids[half:])):
        rows = jnp.concatenate([r[...] for r in group], axis=0)
        part = jnp.dot(g[...], rows, preferred_element_type=F32)
        total = part if total is None else total + part
    out_ref[...] = total.astype(jnp.bfloat16)


def head_call(ga, gb, hids):
    vocab, tokens = ga.shape
    depth = hids[0].shape[-1]
    tile = 1024
    whole = pl.BlockSpec((vocab, tokens), lambda i: (0, 0))
    return pl.pallas_call(
        head_kernel,
        grid=(depth // tile,),
        in_specs=[whole, whole] + [pl.BlockSpec((h.shape[0], tile), lambda i: (0, i)) for h in hids],
        out_specs=pl.BlockSpec((vocab, tile), lambda i: (0, i)),
        out_shape=jax.ShapeDtypeStruct((vocab, depth), jnp.bfloat16),
        compiler_params=pltpu.CompilerParams(vmem_limit_bytes=44 * MIB),
        cost_estimate=pl.CostEstimate(flops=4 * vocab * tokens * depth, bytes_accessed=4 * tokens * depth, transcendentals=0),
    )(ga, gb, *in_hbm(hids))


def local(teacher_hidden, student_hidden, teacher_head, student_head, sampled_ids, valid_mask):
    dp, tensor = lax.axis_index("dp"), lax.axis_index("tensor")
    x, y, core = dp // SIDE, dp % SIDE, tensor % 2
    half = teacher_hidden.shape[0] // 2
    vocab = teacher_head.shape[1]

    ta, sa = teacher_head.T, student_head.T
    tb, sb = send(ta, SIBLING), send(sa, SIBLING)

    shift = jnp.array([o % SIDE for o in OFFSETS], jnp.int32)
    one = (jnp.where(core == 0, x, y) + shift) % SIDE
    two = (jnp.where(core == 0, y, x) + shift) % SIDE
    place = jnp.where(core == 0, one[None, :] * SIDE + two[:, None], two[:, None] * SIDE + one[None, :]).reshape(-1)

    def mine(a):
        return lax.dynamic_index_in_dim(a.reshape(SIDE * SIDE, 2, half), core, 1, keepdims=False)

    ids = jnp.take(mine(sampled_ids), place, axis=0).reshape(SIDE, SIDE * half)
    all_weights = valid_mask.astype(F32)
    token_count = jnp.sum(all_weights)
    weights = mine(all_weights)
    factor = LOSS_SCALE * weights / jnp.sqrt(token_count)
    row_of = flat(x, y, tensor // 2, core) * vocab
    other_of = flat(x, y, tensor // 2, 1 - core) * vocab
    parity = (tensor // 2) % 2
    scalars = jnp.stack([row_of, other_of, parity])

    depth = teacher_hidden.shape[1]
    common, width = depth // 2, depth // 4
    own = lax.dynamic_slice_in_dim(jnp.stack([teacher_hidden, student_hidden]), core * half, half, 1)
    own_x = lax.dynamic_slice_in_dim(own, common + parity * width, width, 2)
    own = jnp.concatenate([own[:, :, :common], own_x], axis=2)
    low, high = send(own, first(1)), send(own, first(-1))
    far_t, far_s = send(low[0], first(1)), send(high[1], first(-1))
    far_t, far_s, tb, sb = lax.optimization_barrier((far_t, far_s, tb, sb))
    heads = (sa, ta, sb, tb)
    row = [own, low, high, jnp.stack([far_t, far_s])]
    row_x = jnp.concatenate([a[:, :, common:] for a in row], axis=1)
    row_c = jnp.concatenate([a[:, :, :common] for a in row], axis=1)
    low_x, high_x = send(row_x, second(1)), send(row_x, second(-1))
    row_y = send(row_x, z_pair())
    low_c, high_c = send(row_c, second(1)), send(row_c, second(-1))
    low_x, high_x, row_y = lax.optimization_barrier((low_x, high_x, row_y))
    far_xt, far_xs = send(low_x[0], second(1)), send(high_x[1], second(-1))
    both_y = send(jnp.stack([low_x, high_x]), z_pair())
    group0, student0 = logits_call(scalars, ids[0:1], [((row_c,), (row_x,), (row_y,))], heads)
    low_c, high_c, both_y, far_xt, far_xs, student0, *group0 = lax.optimization_barrier(
        (low_c, high_c, both_y, far_xt, far_xs, student0, *group0))
    on_t, on_s = low_c[0], high_c[1]
    far_ct, far_cs = send(on_t, second(1)), send(on_s, second(-1))
    far_yt, far_ys = send(far_xt, z_pair()), send(far_xs, z_pair())
    other0 = send(student0, SIBLING)
    group1, group2, student1 = logits_call(scalars, ids[1:3], [
        ((low_c,), (low_x,), (both_y,)), ((high_c,), (high_x,), (both_y,))], heads, (other0,))
    far_ct, far_cs, far_yt, far_ys, student1 = lax.optimization_barrier((far_ct, far_cs, far_yt, far_ys, student1))
    other1 = send(student1, SIBLING)
    group3, student2 = logits_call(scalars, ids[3:4], [((far_ct, far_cs), (far_xt, far_xs), (far_yt, far_ys))], heads, (group1[1],))
    groups = [group0, group1, group2, group3]
    others = [other0, other1, send(student2, SIBLING)]

    total = order_call(place, [g[1] for g in groups])
    for axis in range(3):
        parts = [total, send(total, along(axis, 1)), send(total, along(axis, -1)), send(total, along(axis, 2))]
        if axis < 2:
            total = join_call(parts)
    coef, kl = finish_call(place, factor, weights, parts)

    logits = [g[0] for g in groups]
    away = grad_call(1, scalars, ids, coef, logits, vocab)
    arrived = send(away, SIBLING)
    kept = grad_call(0, scalars, ids, coef, logits, vocab)
    kl = kl + send(kl, SIBLING)
    head_grad = head_call(kept, arrived, [student0, student1, student2] + others).T
    return head_grad, kl[0, 0] / token_count


def solution(mesh):
    placed = (
        P("dp", None),
        P("dp", None),
        P(None, AXES),
        P(None, AXES),
        P(),
        P(),
    )
    return jax.shard_map(
        local,
        mesh=mesh,
        in_specs=placed,
        out_specs=(P(None, AXES), P()),
        check_vma=False,
    )
```

```python
import functools

import jax
import jax.numpy as jnp
from jax import lax
from jax.experimental import pallas as pl
from jax.experimental.pallas import tpu as pltpu
from jax.sharding import PartitionSpec as P

LOSS_SCALE = 64.0
SAMPLED_WEIGHT = 0.0625
SIDE = 4
AXES = ("dp", "tensor")
OFFSETS = (0, -1, 1, 2)
F32 = jnp.float32
MIB = 1 << 20


def flat(x, y, z, c):
    return (((x % SIDE) * SIDE + y % SIDE) * SIDE + z % SIDE) * 2 + c


def pairs(step):
    return [
        (flat(x, y, z, c), flat(*step(x, y, z, c)))
        for x in range(SIDE) for y in range(SIDE) for z in range(SIDE) for c in range(2)
    ]


def first(d):
    return pairs(lambda x, y, z, c: (x + d * (1 - c), y + d * c, z, c))


def second(d):
    return pairs(lambda x, y, z, c: (x + d * c, y + d * (1 - c), z, c))


def along(axis, d):
    return pairs(lambda x, y, z, c: (x + d * (axis == 0), y + d * (axis == 1), z + d * (axis == 2), c))


def z_pair():
    return pairs(lambda x, y, z, c: (x, y, z + 1 - 2 * c, c))


SIBLING = pairs(lambda x, y, z, c: (x, y, z, 1 - c))


def send(array, perm):
    return lax.ppermute(array, AXES, perm)


def nt(a, b):
    return lax.dot_general(a, b, (((1,), (1,)), ((), ())), preferred_element_type=F32)


PAD = -1e30


def stats_of(held, i, first, ids):
    rows, tokens = held.shape[1:]
    step = 40

    def chunk(j, r):
        return held[j, pl.ds(pl.multiple_of(r * step, 8), step), :].reshape(step // 8, 8, tokens)

    def tops(r, carry):
        ms, mt = carry
        return jnp.maximum(ms, jnp.max(chunk(2 * i, r), axis=0)), jnp.maximum(mt, jnp.max(chunk(2 * i + 1, r), axis=0))

    low = jnp.full((8, tokens), PAD, F32)
    ms, mt = lax.fori_loop(0, rows // step, tops, (low, low))
    ms, mt = jnp.max(ms, axis=0, keepdims=True), jnp.max(mt, axis=0, keepdims=True)
    at = lax.broadcasted_iota(jnp.int32, (step, tokens), 0).reshape(step // 8, 8, tokens)
    wanted = ids - first

    def sums(r, carry):
        s, t = chunk(2 * i, r), chunk(2 * i + 1, r)
        u = s - t
        es = jnp.exp(s - ms)
        et = jnp.exp(t - mt)
        picked = jnp.where(at == wanted - r * step, u, 0.0)
        return tuple(c + jnp.sum(v, axis=0) for c, v in zip(carry, (es, et, es * u, picked)))

    nil = jnp.zeros((8, tokens), F32)
    zs, zt, mean, picked = (
        jnp.sum(v, axis=0, keepdims=True) for v in lax.fori_loop(0, rows // step, sums, (nil,) * 4))
    return mt + jnp.log(zt), ms + jnp.log(zs), mean / zs, picked


def add_all(values):
    if len(values) == 4:
        return (values[0] + values[3]) + (values[1] + values[2])
    return sum(values[1:], values[0])


def join(parts):
    def lse(values):
        top = functools.reduce(jnp.maximum, values)
        return top + jnp.log(add_all([jnp.exp(v - top) for v in values]))
    nt_all = lse([p[0] for p in parts])
    ns_all = lse([p[1] for p in parts])
    mean = add_all([jnp.exp(p[1] - ns_all) * p[2] for p in parts])
    return nt_all, ns_all, mean, add_all([p[3] for p in parts])


def logits_kernel(shape, places, scalar_ref, ids_ref, *refs):
    n = len(shape)
    count = sum(len(kind) for group in shape for kind in group)
    pieces, heads, refs = list(refs[:count]), refs[count:count + 4], refs[count + 4:]
    hidden = [[[pieces.pop(0) for _ in kind] for kind in group] for group in shape]
    *outs, student_ref = refs[-7 - 2 * n:-6]
    hid, head, held, in_sems, head_sems, out_sems = refs[-6:]
    vocab, rows = head.shape[1], held.shape[2]
    common, width = hidden[0][0][0].shape[-1], hidden[0][1][0].shape[-1]
    at = (0, pl.multiple_of(common + scalar_ref[2] * width, width), pl.multiple_of(common + (1 - scalar_ref[2]) * width, width))

    def fetch(g, kind, j):
        found = hidden[g][kind]
        source = found[j] if len(found) == 2 else found[0].at[(j,) if len(found[0].shape) == 3 else (places[g], j)]
        return pltpu.make_async_copy(source, hid.at[g, j, :, pl.ds(at[kind], source.shape[-1])], in_sems.at[g, kind, j])

    def fetch_head(h, lo, hi, sem):
        return pltpu.make_async_copy(heads[h].at[:, lo:hi], head.at[h, :, lo:hi], head_sems.at[sem])

    depth = hid.shape[3]
    early = [fetch_head(0, 0, common, 4)] + [fetch(g, 0, 1) for g in range(n)]
    late = [fetch_head(0, common, depth, 0)] + [fetch(g, kind, 1) for g in range(n) for kind in (1, 2)]
    teacher = [fetch_head(1, 0, depth, 1)] + [fetch(g, kind, 0) for g in range(n) for kind in (0, 1, 2)]
    sibling = [[fetch_head(2, 0, depth, 2)], [fetch_head(3, 0, depth, 3)]]

    def start(copies):
        for copy in copies:
            copy.start()

    def wait(copies):
        for copy in copies:
            copy.wait()

    start(early)
    start(late)
    wait(early)
    start(teacher)
    for g in range(n):
        held[g, 0, :vocab, :] = nt(head[0, :, :common], hid[g, 1, :, :common])
    wait(late)
    start(sibling[0])
    for g in range(n):
        held[g, 0, :vocab, :] += nt(head[0, :, common:], hid[g, 1, :, common:])
    wait(teacher)
    start(sibling[1])
    kept = [
        pltpu.make_async_copy(hid.at[g, 1], student_ref.at[pl.ds(g * hid.shape[2], hid.shape[2])], out_sems.at[g, 2])
        for g in range(n)
    ]
    start(kept)
    for g in range(n):
        held[g, 1, :vocab, :] = nt(head[1], hid[g, 0])
    parts, stored = [[] for _ in range(n)], []

    def finish(i):
        for g in range(n):
            held[g, 2 * i:2 * i + 2, vocab:, :] = jnp.full((2, rows - vocab, held.shape[3]), PAD, F32)
            stored.append(pltpu.make_async_copy(
                held.at[g, pl.ds(2 * i, 2)], outs[2 * g].at[pl.ds(2 * i, 2)], out_sems.at[g, i]))
            stored[-1].start()
            parts[g].append(stats_of(held.at[g], i, scalar_ref[i], ids_ref[g:g + 1, :]))

    finish(0)
    for i in range(2):
        wait(sibling[i])
        for g in range(n):
            held[g, 2 + i, :vocab, :] = nt(head[2 + i], hid[g, 1 - i])
    finish(1)
    for g in range(n):
        total = join(parts[g])
        tokens = total[0].shape[1] // SIDE
        for q in range(4):
            for b in range(SIDE):
                outs[2 * g + 1][b, q:q + 1, :] = total[q][:, b * tokens:(b + 1) * tokens]
    wait(kept)
    wait(stored)


def logits_call(scalars, ids, groups, heads, places):
    vocab, depth = heads[0].shape
    n, tokens = ids.shape
    rows = -(-vocab // 40) * 40
    vmem, hbm = pl.BlockSpec(memory_space=pltpu.VMEM), pl.BlockSpec(memory_space=pl.ANY)
    pieces = [a for group in groups for kind in group for a in kind]
    shape = [[[None] * len(kind) for kind in group] for group in groups]
    out = pl.pallas_call(
        functools.partial(logits_kernel, shape, places),
        in_specs=[pl.BlockSpec(memory_space=pltpu.SMEM), vmem] + [hbm] * (len(pieces) + 4),
        out_specs=[pl.BlockSpec(memory_space=pltpu.HBM), vmem] * n + [pl.BlockSpec(memory_space=pltpu.HBM)],
        out_shape=[
            pltpu.HBM((4, rows, tokens), F32),
            jax.ShapeDtypeStruct((SIDE, 4, tokens // SIDE), F32),
        ] * n + [pltpu.HBM((n * tokens, depth), jnp.bfloat16)],
        scratch_shapes=[
            pltpu.VMEM((n, 2, tokens, depth), jnp.bfloat16),
            pltpu.VMEM((4, vocab, depth), jnp.bfloat16),
            pltpu.VMEM((n, 4, rows, tokens), F32),
            pltpu.SemaphoreType.DMA((n, 3, 2)),
            pltpu.SemaphoreType.DMA((5,)),
            pltpu.SemaphoreType.DMA((n, 3)),
        ],
        compiler_params=pltpu.CompilerParams(vmem_limit_bytes=(26 + 9 * n) * MIB),
        cost_estimate=pl.CostEstimate(flops=8 * n * vocab * tokens * depth, bytes_accessed=8 * vocab * depth, transcendentals=0),
    )(scalars, ids, *pieces, *in_hbm(heads))
    return *[out[2 * g:2 * g + 2] for g in range(n)], out[-1]


def order_kernel(place_ref, *refs):
    *groups, out_ref = refs
    for j, group in enumerate(groups):
        for i in range(SIDE):
            b = place_ref[j * SIDE + i]
            for q in range(4):
                out_ref[q, pl.ds(b, 1), :] = group[i, q:q + 1, :]


SMALL = pltpu.CompilerParams(vmem_limit_bytes=4 * MIB)


def order_call(place, groups):
    tokens = groups[0].shape[-1]
    return pl.pallas_call(
        order_kernel,
        in_specs=[pl.BlockSpec(memory_space=pltpu.SMEM)] + [pl.BlockSpec(memory_space=pltpu.VMEM)] * len(groups),
        out_specs=pl.BlockSpec(memory_space=pltpu.VMEM),
        out_shape=jax.ShapeDtypeStruct((4, SIDE * SIDE, tokens), F32),
        compiler_params=SMALL,
    )(place, *groups)


def join_kernel(*refs):
    *ins, out_ref = refs
    total = join([[r[q] for q in range(4)] for r in ins])
    for q in range(4):
        out_ref[q] = total[q]


def join_call(parts):
    vmem = pl.BlockSpec(memory_space=pltpu.VMEM)
    return pl.pallas_call(
        join_kernel,
        in_specs=[vmem] * len(parts),
        out_specs=vmem,
        out_shape=jax.ShapeDtypeStruct(parts[0].shape, F32),
        compiler_params=SMALL,
    )(*parts)


def reads_of(part, ins, held, sems):
    return [pltpu.make_async_copy(ref.at[pl.ds(2 * part, 2)], held.at[j], sems.at[j]) for j, ref in enumerate(ins)]


def write_grads(part, reads, held, scalar_ref, ids_ref, coef_ref, out_ref):
    vocab, tokens = out_ref.shape[0], held.shape[3]
    for j in range(SIDE):
        reads[j].wait()
        s, t = held[j, 0], held[j, 1]
        n_s, factor, shift, pull = (coef_ref[j, q:q + 1, :] for q in range(4))
        rows = lax.broadcasted_iota(jnp.int32, s.shape, 0)
        inner = jnp.exp(s - n_s) * (s - t + shift)
        inner = inner - jnp.where(rows == ids_ref[j:j + 1, :] - scalar_ref[part], pull, 0.0)
        out_ref[:, j * tokens:(j + 1) * tokens] = (factor * inner).astype(jnp.bfloat16)[:vocab]


def finish_kernel(place_ref, scalar_ref, factor_ref, weight_ref, ids_ref, *refs):
    parts, logits = refs[:SIDE], refs[SIDE:2 * SIDE]
    coef_ref, kl_ref, out_ref, rows_ref, held, sems = refs[2 * SIDE:]
    reads = reads_of(1, logits, held, sems)
    for read in reads:
        read.start()
    n_t, n_s, mean, picked = join([[r[q] for q in range(4)] for r in parts])
    kl_ref[...] = jnp.sum(weight_ref[...] * (mean + n_t - n_s), keepdims=True)
    pull = SAMPLED_WEIGHT * -(picked + n_t - n_s)
    for q, value in enumerate((n_s, factor_ref[...], pull - mean, pull)):
        rows_ref[q] = value
    tokens = n_s.shape[1]
    for j in range(SIDE):
        for q in range(4):
            for i in range(SIDE):
                coef_ref[j, q:q + 1, i * tokens:(i + 1) * tokens] = rows_ref[q, pl.ds(place_ref[j * SIDE + i], 1), :]
    write_grads(1, reads, held, scalar_ref, ids_ref, coef_ref, out_ref)


def finish_call(place, scalars, factor, weight, ids, parts, logits, vocab):
    smem, vmem, hbm = (pl.BlockSpec(memory_space=m) for m in (pltpu.SMEM, pltpu.VMEM, pltpu.HBM))
    tokens, rows = factor.shape[1], logits[0].shape[1]
    return pl.pallas_call(
        finish_kernel,
        in_specs=[smem, smem] + [vmem] * (3 + len(parts)) + [hbm] * len(logits),
        out_specs=[vmem, vmem, vmem],
        out_shape=[
            jax.ShapeDtypeStruct((SIDE, 4, SIDE * tokens), F32),
            jax.ShapeDtypeStruct((1, 1), F32),
            jax.ShapeDtypeStruct((vocab, SIDE * SIDE * tokens), jnp.bfloat16),
        ],
        scratch_shapes=[
            pltpu.VMEM((4, SIDE * SIDE, tokens), F32),
            pltpu.VMEM((SIDE, 2, rows, SIDE * tokens), F32),
            pltpu.SemaphoreType.DMA((SIDE,)),
        ],
        compiler_params=pltpu.CompilerParams(vmem_limit_bytes=16 * MIB),
    )(place, scalars, factor, weight, ids, *parts, *in_hbm(logits))


def grad_kernel(part, scalar_ref, ids_ref, coef_ref, *refs):
    *ins, out_ref, held, sems = refs
    reads = reads_of(part, ins, held, sems)
    for read in reads:
        read.start()
    write_grads(part, reads, held, scalar_ref, ids_ref, coef_ref, out_ref)


def in_hbm(arrays):
    return [pltpu.with_memory_space_constraint(a, pltpu.HBM) for a in arrays]


def grad_call(part, scalars, ids, coef, logits, vocab):
    _, rows, tokens = logits[0].shape
    vmem, hbm = pl.BlockSpec(memory_space=pltpu.VMEM), pl.BlockSpec(memory_space=pltpu.HBM)
    return pl.pallas_call(
        functools.partial(grad_kernel, part),
        in_specs=[pl.BlockSpec(memory_space=pltpu.SMEM), vmem, vmem] + [hbm] * SIDE,
        out_specs=vmem,
        out_shape=jax.ShapeDtypeStruct((vocab, SIDE * tokens), jnp.bfloat16),
        scratch_shapes=[pltpu.VMEM((SIDE, 2, rows, tokens), F32), pltpu.SemaphoreType.DMA((SIDE,))],
        compiler_params=pltpu.CompilerParams(vmem_limit_bytes=16 * MIB),
        cost_estimate=pl.CostEstimate(flops=10 * vocab * tokens * SIDE, bytes_accessed=10 * vocab * tokens * SIDE, transcendentals=0),
    )(scalars, ids, coef, *in_hbm(logits))


def head_kernel(kla_ref, klb_ref, ga_ref, gb_ref, *refs):
    *hids, out_ref, kl_ref = refs

    @pl.when(pl.program_id(0) == 0)
    def _():
        kl_ref[...] = kla_ref[...] + klb_ref[...]

    half = len(hids) // 2
    total = None
    for g, group in ((ga_ref, hids[:half]), (gb_ref, hids[half:])):
        rows = jnp.concatenate([r[...] for r in group], axis=0)
        part = jnp.dot(g[...], rows, preferred_element_type=F32)
        total = part if total is None else total + part
    out_ref[...] = total.astype(jnp.bfloat16)


def head_call(kls, ga, gb, hids):
    vocab, tokens = ga.shape
    depth = hids[0].shape[-1]
    tile = 1024
    whole = pl.BlockSpec((vocab, tokens), lambda i: (0, 0))
    one = pl.BlockSpec((1, 1), lambda i: (0, 0))
    return pl.pallas_call(
        head_kernel,
        grid=(depth // tile,),
        in_specs=[one, one, whole, whole] + [pl.BlockSpec((h.shape[0], tile), lambda i: (0, i)) for h in hids],
        out_specs=[pl.BlockSpec((vocab, tile), lambda i: (0, i)), one],
        out_shape=[jax.ShapeDtypeStruct((vocab, depth), jnp.bfloat16), jax.ShapeDtypeStruct((1, 1), F32)],
        compiler_params=pltpu.CompilerParams(vmem_limit_bytes=44 * MIB),
        cost_estimate=pl.CostEstimate(flops=4 * vocab * tokens * depth, bytes_accessed=4 * tokens * depth, transcendentals=0),
    )(*kls, ga, gb, *in_hbm(hids))


def local(teacher_hidden, student_hidden, teacher_head, student_head, sampled_ids, valid_mask):
    dp, tensor = lax.axis_index("dp"), lax.axis_index("tensor")
    x, y, core = dp // SIDE, dp % SIDE, tensor % 2
    half = teacher_hidden.shape[0] // 2
    vocab = teacher_head.shape[1]

    ta, sa = teacher_head.T, student_head.T
    tb, sb = send(ta, SIBLING), send(sa, SIBLING)

    shift = jnp.array([o % SIDE for o in OFFSETS], jnp.int32)
    one = (jnp.where(core == 0, x, y) + shift) % SIDE
    two = (jnp.where(core == 0, y, x) + shift) % SIDE
    place = jnp.where(core == 0, one[None, :] * SIDE + two[:, None], two[:, None] * SIDE + one[None, :]).reshape(-1)

    def mine(a):
        return lax.dynamic_index_in_dim(a.reshape(SIDE * SIDE, 2, half), core, 1, keepdims=False)

    ids = jnp.take(mine(sampled_ids), place, axis=0).reshape(SIDE, SIDE * half)
    all_weights = valid_mask.astype(F32)
    token_count = jnp.sum(all_weights)
    weights = mine(all_weights)
    factor = LOSS_SCALE * weights / jnp.sqrt(token_count)
    weights = weights / token_count
    row_of = flat(x, y, tensor // 2, core) * vocab
    other_of = flat(x, y, tensor // 2, 1 - core) * vocab
    parity = (tensor // 2) % 2
    scalars = jnp.stack([row_of, other_of, parity])

    depth = teacher_hidden.shape[1]
    common, width = depth // 2, depth // 4
    own = lax.dynamic_slice_in_dim(jnp.stack([teacher_hidden, student_hidden]), core * half, half, 1)
    own_x = lax.dynamic_slice_in_dim(own, common + parity * width, width, 2)
    own = jnp.concatenate([own[:, :, :common], own_x], axis=2)
    low, high = send(own, first(1)), send(own, first(-1))
    far_t, far_s = send(low[0], first(1)), send(high[1], first(-1))
    far_t, far_s, tb, sb = lax.optimization_barrier((far_t, far_s, tb, sb))
    heads = (sa, ta, sb, tb)
    row = [own, low, high, jnp.stack([far_t, far_s])]
    row_x = jnp.concatenate([a[:, :, common:] for a in row], axis=1)
    row_x, *row = lax.optimization_barrier((row_x, *row))
    row_c = jnp.concatenate([a[:, :, :common] for a in row], axis=1)
    low_x, high_x = send(row_x, second(1)), send(row_x, second(-1))
    row_y = send(row_x, z_pair())
    low_c, high_c = send(row_c, second(1)), send(row_c, second(-1))
    low_x, high_x, row_y = lax.optimization_barrier((low_x, high_x, row_y))
    far_xt, far_xs = send(low_x[0], second(1)), send(high_x[1], second(-1))
    both_y = send(jnp.stack([low_x, high_x]), z_pair())
    low_c, high_c, far_xt, far_xs = lax.optimization_barrier((low_c, high_c, far_xt, far_xs))
    on_t, on_s = low_c[0], high_c[1]
    far_ct, far_cs = send(on_t, second(1)), send(on_s, second(-1))
    both_y, on_t, on_s = lax.optimization_barrier((both_y, on_t, on_s))
    far_yt, far_ys = send(far_xt, z_pair()), send(far_xs, z_pair())
    group0, group1, student0 = logits_call(
        scalars, ids[0:2], [((row_c,), (row_x,), (row_y,)), ((low_c,), (low_x,), (both_y,))], heads, (0, 0))
    far_ct, far_cs, far_yt, far_ys, student0 = lax.optimization_barrier((far_ct, far_cs, far_yt, far_ys, student0))
    other0 = send(student0, SIBLING)
    group2, group3, student1 = logits_call(
        scalars, ids[2:4],
        [((high_c,), (high_x,), (both_y,)), ((far_ct, far_cs), (far_xt, far_xs), (far_yt, far_ys))], heads, (1, 0))
    groups = [group0, group1, group2, group3]
    others = [other0, send(student1, SIBLING)]

    total = order_call(place, [g[1] for g in groups])
    for axis in range(3):
        parts = [total, send(total, along(axis, 1)), send(total, along(axis, -1)), send(total, along(axis, 2))]
        if axis < 2:
            total = join_call(parts)
    logits = [g[0] for g in groups]
    coef, kl, away = finish_call(place, scalars, factor, weights, ids, parts, logits, vocab)
    arrived = send(away, SIBLING)
    other_kl = send(kl, SIBLING)
    kept = grad_call(0, scalars, ids, coef, logits, vocab)
    head_grad, kl = head_call((kl, other_kl), kept, arrived, [student0, student1] + others)
    return head_grad.T, kl.reshape(())


def solution(mesh):
    placed = (
        P("dp", None),
        P("dp", None),
        P(None, AXES),
        P(None, AXES),
        P(),
        P(),
    )
    return jax.shard_map(
        local,
        mesh=mesh,
        in_specs=placed,
        out_specs=(P(None, AXES), P()),
        check_vma=False,
    )
```

```python
import functools

import jax
import jax.numpy as jnp
from jax import lax
from jax.experimental import pallas as pl
from jax.experimental.pallas import tpu as pltpu
from jax.sharding import PartitionSpec as P

LOSS_SCALE = 64.0
SAMPLED_WEIGHT = 0.0625
SIDE = 4
AXES = ("dp", "tensor")
OFFSETS = (0, -1, 1, 2)
F32 = jnp.float32
MIB = 1 << 20


def flat(x, y, z, c):
    return (((x % SIDE) * SIDE + y % SIDE) * SIDE + z % SIDE) * 2 + c


def pairs(step):
    return [
        (flat(x, y, z, c), flat(*step(x, y, z, c)))
        for x in range(SIDE) for y in range(SIDE) for z in range(SIDE) for c in range(2)
    ]


def first(d):
    return pairs(lambda x, y, z, c: (x + d * (1 - c), y + d * c, z, c))


def second(d):
    return pairs(lambda x, y, z, c: (x + d * c, y + d * (1 - c), z, c))


def along(axis, d):
    return pairs(lambda x, y, z, c: (x + d * (axis == 0), y + d * (axis == 1), z + d * (axis == 2), c))


def z_pair():
    return pairs(lambda x, y, z, c: (x, y, z + 1 - 2 * c, c))


SIBLING = pairs(lambda x, y, z, c: (x, y, z, 1 - c))


def send(array, perm):
    return lax.ppermute(array, AXES, perm)


def nt(a, b):
    return lax.dot_general(a, b, (((1,), (1,)), ((), ())), preferred_element_type=F32)


PAD = -1e30


def stats_of(held, i, first, ids):
    rows, tokens = held.shape[1:]
    step = 40

    def chunk(j, r):
        return held[j, pl.ds(pl.multiple_of(r * step, 8), step), :].reshape(step // 8, 8, tokens)

    def tops(r, carry):
        ms, mt = carry
        return jnp.maximum(ms, jnp.max(chunk(2 * i, r), axis=0)), jnp.maximum(mt, jnp.max(chunk(2 * i + 1, r), axis=0))

    low = jnp.full((8, tokens), PAD, F32)
    ms, mt = lax.fori_loop(0, rows // step, tops, (low, low))
    ms, mt = jnp.max(ms, axis=0, keepdims=True), jnp.max(mt, axis=0, keepdims=True)
    at = lax.broadcasted_iota(jnp.int32, (step, tokens), 0).reshape(step // 8, 8, tokens)
    wanted = ids - first

    def sums(r, carry):
        s, t = chunk(2 * i, r), chunk(2 * i + 1, r)
        u = s - t
        es = jnp.exp(s - ms)
        et = jnp.exp(t - mt)
        picked = jnp.where(at == wanted - r * step, u, 0.0)
        return tuple(c + jnp.sum(v, axis=0) for c, v in zip(carry, (es, et, es * u, picked)))

    nil = jnp.zeros((8, tokens), F32)
    zs, zt, mean, picked = (
        jnp.sum(v, axis=0, keepdims=True) for v in lax.fori_loop(0, rows // step, sums, (nil,) * 4))
    return mt + jnp.log(zt), ms + jnp.log(zs), mean / zs, picked


def add_all(values):
    if len(values) == 4:
        return (values[0] + values[3]) + (values[1] + values[2])
    return sum(values[1:], values[0])


def join(parts):
    def lse(values):
        top = functools.reduce(jnp.maximum, values)
        return top + jnp.log(add_all([jnp.exp(v - top) for v in values]))
    nt_all = lse([p[0] for p in parts])
    ns_all = lse([p[1] for p in parts])
    mean = add_all([jnp.exp(p[1] - ns_all) * p[2] for p in parts])
    return nt_all, ns_all, mean, add_all([p[3] for p in parts])


def logits_kernel(shape, places, scalar_ref, ids_ref, *refs):
    n = len(shape)
    count = sum(len(kind) for group in shape for kind in group)
    pieces, heads, refs = list(refs[:count]), refs[count:count + 4], refs[count + 4:]
    hidden = [[[pieces.pop(0) for _ in kind] for kind in group] for group in shape]
    *outs, student_ref = refs[-7 - 2 * n:-6]
    hid, head, held, in_sems, head_sems, out_sems = refs[-6:]
    vocab, rows = head.shape[1], held.shape[2]
    common, width = hidden[0][0][0].shape[-1], hidden[0][1][0].shape[-1]
    at = (0, pl.multiple_of(common + scalar_ref[2] * width, width), pl.multiple_of(common + (1 - scalar_ref[2]) * width, width))

    def fetch(g, kind, j):
        found = hidden[g][kind]
        source = found[j] if len(found) == 2 else found[0].at[(j,) if len(found[0].shape) == 3 else (places[g], j)]
        return pltpu.make_async_copy(source, hid.at[g, j, :, pl.ds(at[kind], source.shape[-1])], in_sems.at[g, kind, j])

    def fetch_head(h, lo, hi, sem):
        return pltpu.make_async_copy(heads[h].at[:, lo:hi], head.at[h, :, lo:hi], head_sems.at[sem])

    depth = hid.shape[3]
    early = [fetch_head(0, 0, common, 4)] + [fetch(g, 0, 1) for g in range(n)]
    late = [fetch_head(0, common, depth, 0)] + [fetch(g, kind, 1) for g in range(n) for kind in (1, 2)]
    teacher = [fetch_head(1, 0, depth, 1)] + [fetch(g, kind, 0) for g in range(n) for kind in (0, 1, 2)]
    sibling = [[fetch_head(2, 0, depth, 2)], [fetch_head(3, 0, depth, 3)]]

    def start(copies):
        for copy in copies:
            copy.start()

    def wait(copies):
        for copy in copies:
            copy.wait()

    start(early)
    start(late)
    wait(early)
    start(teacher)
    for g in range(n):
        held[g, 0, :vocab, :] = nt(head[0, :, :common], hid[g, 1, :, :common])
    wait(late)
    start(sibling[0])
    for g in range(n):
        held[g, 0, :vocab, :] += nt(head[0, :, common:], hid[g, 1, :, common:])
    wait(teacher)
    start(sibling[1])
    kept = [
        pltpu.make_async_copy(hid.at[g, 1], student_ref.at[pl.ds(g * hid.shape[2], hid.shape[2])], out_sems.at[g, 2])
        for g in range(n)
    ]
    start(kept)
    for g in range(n):
        held[g, 1, :vocab, :] = nt(head[1], hid[g, 0])
    parts, stored = [[] for _ in range(n)], []

    def finish(i):
        for g in range(n):
            held[g, 2 * i:2 * i + 2, vocab:, :] = jnp.full((2, rows - vocab, held.shape[3]), PAD, F32)
            stored.append(pltpu.make_async_copy(
                held.at[g, pl.ds(2 * i, 2)], outs[2 * g].at[pl.ds(2 * i, 2)], out_sems.at[g, i]))
            stored[-1].start()
            parts[g].append(stats_of(held.at[g], i, scalar_ref[i], ids_ref[g:g + 1, :]))

    finish(0)
    for i in range(2):
        wait(sibling[i])
        for g in range(n):
            held[g, 2 + i, :vocab, :] = nt(head[2 + i], hid[g, 1 - i])
    finish(1)
    for g in range(n):
        total = join(parts[g])
        tokens = total[0].shape[1] // SIDE
        for q in range(4):
            for b in range(SIDE):
                outs[2 * g + 1][b, q:q + 1, :] = total[q][:, b * tokens:(b + 1) * tokens]
    wait(kept)
    wait(stored)


def logits_call(scalars, ids, groups, heads, places):
    vocab, depth = heads[0].shape
    n, tokens = ids.shape
    rows = -(-vocab // 40) * 40
    vmem, hbm = pl.BlockSpec(memory_space=pltpu.VMEM), pl.BlockSpec(memory_space=pl.ANY)
    pieces = [a for group in groups for kind in group for a in kind]
    shape = [[[None] * len(kind) for kind in group] for group in groups]
    out = pl.pallas_call(
        functools.partial(logits_kernel, shape, places),
        in_specs=[pl.BlockSpec(memory_space=pltpu.SMEM), vmem] + [hbm] * (len(pieces) + 4),
        out_specs=[pl.BlockSpec(memory_space=pltpu.HBM), vmem] * n + [pl.BlockSpec(memory_space=pltpu.HBM)],
        out_shape=[
            pltpu.HBM((4, rows, tokens), F32),
            jax.ShapeDtypeStruct((SIDE, 4, tokens // SIDE), F32),
        ] * n + [pltpu.HBM((n * tokens, depth), jnp.bfloat16)],
        scratch_shapes=[
            pltpu.VMEM((n, 2, tokens, depth), jnp.bfloat16),
            pltpu.VMEM((4, vocab, depth), jnp.bfloat16),
            pltpu.VMEM((n, 4, rows, tokens), F32),
            pltpu.SemaphoreType.DMA((n, 3, 2)),
            pltpu.SemaphoreType.DMA((5,)),
            pltpu.SemaphoreType.DMA((n, 3)),
        ],
        compiler_params=pltpu.CompilerParams(vmem_limit_bytes=(26 + 9 * n) * MIB),
        cost_estimate=pl.CostEstimate(flops=8 * n * vocab * tokens * depth, bytes_accessed=8 * vocab * depth, transcendentals=0),
    )(scalars, ids, *pieces, *in_hbm(heads))
    return *[out[2 * g:2 * g + 2] for g in range(n)], out[-1]


def order_kernel(place_ref, *refs):
    *groups, out_ref = refs
    for j, group in enumerate(groups):
        for i in range(SIDE):
            b = place_ref[j * SIDE + i]
            for q in range(4):
                out_ref[q, pl.ds(b, 1), :] = group[i, q:q + 1, :]


SMALL = pltpu.CompilerParams(vmem_limit_bytes=4 * MIB)


def order_call(place, groups):
    tokens = groups[0].shape[-1]
    return pl.pallas_call(
        order_kernel,
        in_specs=[pl.BlockSpec(memory_space=pltpu.SMEM)] + [pl.BlockSpec(memory_space=pltpu.VMEM)] * len(groups),
        out_specs=pl.BlockSpec(memory_space=pltpu.VMEM),
        out_shape=jax.ShapeDtypeStruct((4, SIDE * SIDE, tokens), F32),
        compiler_params=SMALL,
    )(place, *groups)


def join_kernel(*refs):
    *ins, out_ref = refs
    total = join([[r[q] for q in range(4)] for r in ins])
    for q in range(4):
        out_ref[q] = total[q]


def join_call(parts):
    vmem = pl.BlockSpec(memory_space=pltpu.VMEM)
    return pl.pallas_call(
        join_kernel,
        in_specs=[vmem] * len(parts),
        out_specs=vmem,
        out_shape=jax.ShapeDtypeStruct(parts[0].shape, F32),
        compiler_params=SMALL,
    )(*parts)


def reads_of(part, ins, held, sems):
    return [pltpu.make_async_copy(ref.at[pl.ds(2 * part, 2)], held.at[j], sems.at[j]) for j, ref in enumerate(ins)]


def write_grads(part, reads, held, scalar_ref, ids_ref, coef_ref, out_ref):
    vocab, tokens = out_ref.shape[0], held.shape[3]
    for j in range(SIDE):
        reads[j].wait()
        s, t = held[j, 0], held[j, 1]
        n_s, factor, shift, pull = (coef_ref[j, q:q + 1, :] for q in range(4))
        rows = lax.broadcasted_iota(jnp.int32, s.shape, 0)
        inner = jnp.exp(s - n_s) * (s - t + shift)
        inner = inner - jnp.where(rows == ids_ref[j:j + 1, :] - scalar_ref[part], pull, 0.0)
        out_ref[:, j * tokens:(j + 1) * tokens] = (factor * inner).astype(jnp.bfloat16)[:vocab]


def finish_kernel(place_ref, scalar_ref, factor_ref, weight_ref, ids_ref, *refs):
    parts, logits = refs[:SIDE], refs[SIDE:2 * SIDE]
    coef_ref, kl_ref, out_ref, rows_ref, held, sems = refs[2 * SIDE:]
    reads = reads_of(1, logits, held, sems)
    for read in reads:
        read.start()
    n_t, n_s, mean, picked = join([[r[q] for q in range(4)] for r in parts])
    kl_ref[...] = jnp.sum(weight_ref[...] * (mean + n_t - n_s), keepdims=True)
    pull = SAMPLED_WEIGHT * -(picked + n_t - n_s)
    for q, value in enumerate((n_s, factor_ref[...], pull - mean, pull)):
        rows_ref[q] = value
    tokens = n_s.shape[1]
    for j in range(SIDE):
        for q in range(4):
            for i in range(SIDE):
                coef_ref[j, q:q + 1, i * tokens:(i + 1) * tokens] = rows_ref[q, pl.ds(place_ref[j * SIDE + i], 1), :]
    write_grads(1, reads, held, scalar_ref, ids_ref, coef_ref, out_ref)


def finish_call(place, scalars, factor, weight, ids, parts, logits, vocab):
    smem, vmem, hbm = (pl.BlockSpec(memory_space=m) for m in (pltpu.SMEM, pltpu.VMEM, pltpu.HBM))
    tokens, rows = factor.shape[1], logits[0].shape[1]
    return pl.pallas_call(
        finish_kernel,
        in_specs=[smem, smem] + [vmem] * (3 + len(parts)) + [hbm] * len(logits),
        out_specs=[vmem, vmem, vmem],
        out_shape=[
            jax.ShapeDtypeStruct((SIDE, 4, SIDE * tokens), F32),
            jax.ShapeDtypeStruct((1, 1), F32),
            jax.ShapeDtypeStruct((vocab, SIDE * SIDE * tokens), jnp.bfloat16),
        ],
        scratch_shapes=[
            pltpu.VMEM((4, SIDE * SIDE, tokens), F32),
            pltpu.VMEM((SIDE, 2, rows, SIDE * tokens), F32),
            pltpu.SemaphoreType.DMA((SIDE,)),
        ],
        compiler_params=pltpu.CompilerParams(vmem_limit_bytes=16 * MIB),
    )(place, scalars, factor, weight, ids, *parts, *in_hbm(logits))


def grad_kernel(part, scalar_ref, ids_ref, coef_ref, *refs):
    *ins, out_ref, held, sems = refs
    reads = reads_of(part, ins, held, sems)
    for read in reads:
        read.start()
    write_grads(part, reads, held, scalar_ref, ids_ref, coef_ref, out_ref)


def in_hbm(arrays):
    return [pltpu.with_memory_space_constraint(a, pltpu.HBM) for a in arrays]


def grad_call(part, scalars, ids, coef, logits, vocab):
    _, rows, tokens = logits[0].shape
    vmem, hbm = pl.BlockSpec(memory_space=pltpu.VMEM), pl.BlockSpec(memory_space=pltpu.HBM)
    return pl.pallas_call(
        functools.partial(grad_kernel, part),
        in_specs=[pl.BlockSpec(memory_space=pltpu.SMEM), vmem, vmem] + [hbm] * SIDE,
        out_specs=vmem,
        out_shape=jax.ShapeDtypeStruct((vocab, SIDE * tokens), jnp.bfloat16),
        scratch_shapes=[pltpu.VMEM((SIDE, 2, rows, tokens), F32), pltpu.SemaphoreType.DMA((SIDE,))],
        compiler_params=pltpu.CompilerParams(vmem_limit_bytes=16 * MIB),
        cost_estimate=pl.CostEstimate(flops=10 * vocab * tokens * SIDE, bytes_accessed=10 * vocab * tokens * SIDE, transcendentals=0),
    )(scalars, ids, coef, *in_hbm(logits))


def head_kernel(kla_ref, klb_ref, ga_ref, gb_ref, *refs):
    *hids, out_ref, kl_ref = refs

    @pl.when(pl.program_id(0) == 0)
    def _():
        kl_ref[...] = kla_ref[...] + klb_ref[...]

    half = len(hids) // 2
    total = None
    for g, group in ((ga_ref, hids[:half]), (gb_ref, hids[half:])):
        rows = jnp.concatenate([r[...] for r in group], axis=0)
        part = jnp.dot(g[...], rows, preferred_element_type=F32)
        total = part if total is None else total + part
    out_ref[...] = total.astype(jnp.bfloat16)


def head_call(kls, ga, gb, hids):
    vocab, tokens = ga.shape
    depth = hids[0].shape[-1]
    tile = 1024
    whole = pl.BlockSpec((vocab, tokens), lambda i: (0, 0))
    one = pl.BlockSpec((1, 1), lambda i: (0, 0))
    return pl.pallas_call(
        head_kernel,
        grid=(depth // tile,),
        in_specs=[one, one, whole, whole] + [pl.BlockSpec((h.shape[0], tile), lambda i: (0, i)) for h in hids],
        out_specs=[pl.BlockSpec((vocab, tile), lambda i: (0, i)), one],
        out_shape=[jax.ShapeDtypeStruct((vocab, depth), jnp.bfloat16), jax.ShapeDtypeStruct((1, 1), F32)],
        compiler_params=pltpu.CompilerParams(vmem_limit_bytes=44 * MIB),
        cost_estimate=pl.CostEstimate(flops=4 * vocab * tokens * depth, bytes_accessed=4 * tokens * depth, transcendentals=0),
    )(*kls, ga, gb, *in_hbm(hids))


def local(teacher_hidden, student_hidden, teacher_head, student_head, sampled_ids, valid_mask):
    dp, tensor = lax.axis_index("dp"), lax.axis_index("tensor")
    x, y, core = dp // SIDE, dp % SIDE, tensor % 2
    half = teacher_hidden.shape[0] // 2
    vocab = teacher_head.shape[1]

    ta, sa = teacher_head.T, student_head.T
    tb, sb = send(ta, SIBLING), send(sa, SIBLING)

    shift = jnp.array([o % SIDE for o in OFFSETS], jnp.int32)
    one = (jnp.where(core == 0, x, y) + shift) % SIDE
    two = (jnp.where(core == 0, y, x) + shift) % SIDE
    place = jnp.where(core == 0, one[None, :] * SIDE + two[:, None], two[:, None] * SIDE + one[None, :]).reshape(-1)

    def mine(a):
        return lax.dynamic_index_in_dim(a.reshape(SIDE * SIDE, 2, half), core, 1, keepdims=False)

    ids = jnp.take(mine(sampled_ids), place, axis=0).reshape(SIDE, SIDE * half)
    all_weights = valid_mask.astype(F32)
    token_count = jnp.sum(all_weights)
    weights = mine(all_weights)
    factor = LOSS_SCALE * weights / jnp.sqrt(token_count)
    weights = weights / token_count
    row_of = flat(x, y, tensor // 2, core) * vocab
    other_of = flat(x, y, tensor // 2, 1 - core) * vocab
    parity = (tensor // 2) % 2
    scalars = jnp.stack([row_of, other_of, parity])

    depth = teacher_hidden.shape[1]
    common, width = depth // 2, depth // 4
    own = lax.dynamic_slice_in_dim(jnp.stack([teacher_hidden, student_hidden]), core * half, half, 1)
    own_x = lax.dynamic_slice_in_dim(own, common + parity * width, width, 2)
    own = jnp.concatenate([own[:, :, :common], own_x], axis=2)
    low, high = send(own, first(1)), send(own, first(-1))
    far_t, far_s = send(low[0], first(1)), send(high[1], first(-1))
    far_t, far_s, tb, sb = lax.optimization_barrier((far_t, far_s, tb, sb))
    heads = (sa, ta, sb, tb)
    row = [own, low, high, jnp.stack([far_t, far_s])]
    row_x = jnp.concatenate([a[:, :, common:] for a in row], axis=1)
    row_x, *row = lax.optimization_barrier((row_x, *row))
    row_c = jnp.concatenate([a[:, :, :common] for a in row], axis=1)
    low_x, high_x = send(row_x, second(1)), send(row_x, second(-1))
    row_y = send(row_x, z_pair())
    low_c, high_c = send(row_c, second(1)), send(row_c, second(-1))
    low_x, high_x, row_y = lax.optimization_barrier((low_x, high_x, row_y))
    far_xt, far_xs = send(low_x[0], second(1)), send(high_x[1], second(-1))
    both_y = send(jnp.stack([low_x, high_x]), z_pair())
    low_c, high_c, far_xt, far_xs = lax.optimization_barrier((low_c, high_c, far_xt, far_xs))
    on_t, on_s = low_c[0], high_c[1]
    far_ct, far_cs = send(on_t, second(1)), send(on_s, second(-1))
    both_y, on_t, on_s = lax.optimization_barrier((both_y, on_t, on_s))
    far_y = send(jnp.stack([far_xt, far_xs]), z_pair())
    group0, group1, student0 = logits_call(
        scalars, ids[0:2], [((row_c,), (row_x,), (row_y,)), ((low_c,), (low_x,), (both_y,))], heads, (0, 0))
    far_ct, far_cs, far_y, student0 = lax.optimization_barrier((far_ct, far_cs, far_y, student0))
    other0 = send(student0, SIBLING)
    group2, group3, student1 = logits_call(
        scalars, ids[2:4],
        [((high_c,), (high_x,), (both_y,)), ((far_ct, far_cs), (far_xt, far_xs), (far_y,))], heads, (1, 0))
    groups = [group0, group1, group2, group3]
    others = [other0, send(student1, SIBLING)]

    total = order_call(place, [g[1] for g in groups])
    for axis in range(3):
        parts = [total, send(total, along(axis, 1)), send(total, along(axis, -1)), send(total, along(axis, 2))]
        if axis < 2:
            total = join_call(parts)
    logits = [g[0] for g in groups]
    coef, kl, away = finish_call(place, scalars, factor, weights, ids, parts, logits, vocab)
    arrived = send(away, SIBLING)
    other_kl = send(kl, SIBLING)
    kept = grad_call(0, scalars, ids, coef, logits, vocab)
    head_grad, kl = head_call((kl, other_kl), kept, arrived, [student0, student1] + others)
    return head_grad.T, kl.reshape(())


def solution(mesh):
    placed = (
        P("dp", None),
        P("dp", None),
        P(None, AXES),
        P(None, AXES),
        P(),
        P(),
    )
    return jax.shard_map(
        local,
        mesh=mesh,
        in_specs=placed,
        out_specs=(P(None, AXES), P()),
        check_vma=False,
    )
```
